512 devices in a mesh: row: 16 (over x_hi, y, core), col: 32 (over x_lo, z).
Axes of the slice: x: 4 (x_hi: 2, x_lo: 2; x = x_hi * 2 + x_lo), y: 4, z: 16, core: 2. Of those that a mesh axis runs over, the one named last changes fastest.
Arguments:
- grads: bfloat16 [4096, 8192], P('row', 'col'), may hold values from -64 to 64
Outputs:
- kernel: float32 [4096, 4096], P('row', 'col')
The draws below stay inside these ranges and needn't reach their ends.
All inputs are finite; a program needn't handle non-finite values.
Results may differ from the reference program's by a relative error of at most 0.002.
Values may be sent and summed in bfloat16 or wider, within the bound.
A program may use at most 64 MiB of HBM per device.

```python
import math
import jax
import jax.numpy as jnp
from jax import lax

K = 8192
BW = 64
N_EX = 4096


def draw_grads(key, part):
    keys = jax.random.split(key, 4)
    layers = K // BW
    noise = jax.random.normal(keys[0], (N_EX, layers, BW), jnp.float32)
    mixing = jnp.eye(BW, dtype=jnp.float32)[None] + 0.6 * jax.random.normal(keys[1], (layers, BW, BW), jnp.float32) / math.sqrt(BW)
    column_scale = jnp.exp(jax.random.uniform(keys[2], (layers, BW), jnp.float32, 0.0, math.log(10.0)))
    row_scale = jnp.exp(jax.random.uniform(keys[3], (N_EX, 1, 1), jnp.float32, math.log(0.5), math.log(2.0)))
    values = jnp.einsum('nlb,lbc->nlc', noise, mixing) * column_scale[None] * row_scale
    return jnp.clip(values, -64.0, 64.0).reshape(N_EX, K).astype(jnp.bfloat16)


def setup_inputs(seed: int = 0) -> dict:
    arg_keys = jax.random.split(jax.random.key(seed), 2)
    grads = draw_grads(jax.random.fold_in(arg_keys[1], 71), 0)
    return dict(grads=grads)


def factor(total, count):
    width = total.shape[-1]
    unit = jnp.eye(width, dtype=jnp.float32)
    fisher = total / count + 0.1 * unit
    lower = jnp.linalg.cholesky(fisher)
    return jax.vmap(lambda matrix: jax.scipy.linalg.solve_triangular(matrix, unit, lower=True))(lower)

def reference(grads):
    count = grads.shape[0]
    layers = grads.reshape(count, K // BW, BW).astype(jnp.float32)
    total = jnp.einsum('nlb,nlc->lbc', layers, layers, precision=lax.Precision.HIGHEST)
    inverse = factor(total, count)
    whitened = jnp.einsum('nlb,lcb->nlc', layers, inverse, precision=lax.Precision.HIGHEST)
    whitened = whitened.astype(jnp.bfloat16).reshape(count, K)
    kernel = jnp.dot(whitened.astype(jnp.float32), whitened.T.astype(jnp.float32), preferred_element_type=jnp.float32)
    return kernel * K ** (-0.5)
```

```python
import functools

import jax
import jax.numpy as jnp
from jax import lax
from jax.experimental import pallas as pl
from jax.experimental.pallas import tpu as pltpu
from jax.sharding import PartitionSpec as P

BW = 64
F32 = jnp.float32
BF16 = jnp.bfloat16
MESH = pl.DeviceIdType.MESH
NT = (((1,), (1,)), ((), ()))
TN = (((0,), (0,)), ((), ()))


def eliminate(blocks, inverse, start):
    lane = lax.broadcasted_iota(jnp.int32, (1, 1, 8, 128), 3)
    sub = lax.broadcasted_iota(jnp.int32, (1, 1, 8, 128), 2)
    place = lax.broadcasted_iota(jnp.int32, (8, 1, 8, 128), 0)
    low = lane < BW
    for j in range(8):
        row = blocks[0:1, :, j : j + 1, :]
        other = inverse[0:1, :, j : j + 1, :]
        column = jnp.where(low, blocks[:, :, :, j : j + 1], blocks[:, :, :, BW + j : BW + j + 1])
        pivot = jnp.where(low[:, :, 0:1], row[:, :, :, j : j + 1], row[:, :, :, BW + j : BW + j + 1])
        below = ((place == 0) & (sub > j)) | ((place > 0) & (place + start < 8))
        factor = jnp.where(below, column / pivot, 0.0)
        blocks = blocks - factor * row
        inverse = inverse - factor * other
        scale = jnp.where((place == 0) & (sub == j), lax.rsqrt(pivot), 1.0)
        inverse = inverse * scale
    return blocks, inverse


def rotate(blocks):
    return jnp.concatenate([blocks[1:], blocks[:1]], axis=0)


def kernel(
    n,
    g_ref,
    out_ref,
    rows,
    cols,
    fsend,
    frecv,
    full,
    linv,
    inv,
    part,
    precv,
    ring_send,
    ring_recv,
    col_send,
    col_recv,
    colg_send,
    colg_recv,
    colx_send,
    colx_recv,
    rs_send,
    rs_recv,
    ag_send,
    ag_recv,
    ze_send,
    ze_recv,
    ig_send,
    ig_recv,
    ix_send,
    ix_recv,
    p_send,
    p_recv,
):
    r = lax.axis_index("row")
    c = lax.axis_index("col")
    half = n // 2
    x_lo = c // n
    z = lax.rem(c, n)
    x_hi = r // half
    pair = r // 2
    core = lax.rem(r, 2)
    base = x_lo * n
    depth = 128 // n

    def at(row, plane):
        return {"row": row, "col": base + plane}

    barrier = pltpu.get_barrier_semaphore()

    def greet(d, _):
        pl.semaphore_signal(barrier, 1, device_id=at(lax.rem(r + d, n), z), device_id_type=MESH)
        pl.semaphore_signal(barrier, 1, device_id=at(r, lax.rem(z + d, n)), device_id_type=MESH)
        return 0

    lax.fori_loop(1, n, greet, 0)
    pl.semaphore_signal(
        barrier, 1, device_id={"row": r, "col": (1 - x_lo) * n + z}, device_id_type=MESH
    )
    for k in range(2):
        source = k * half + z // 2
        away = (source != r) | (r != z)

        @pl.when(away)
        def _(source=source):
            pl.semaphore_signal(barrier, 1, device_id=at(source, r), device_id_type=MESH)

    elsewhere = 0
    for h in range(2):
        target = 2 * lax.rem(r, half) + h
        elsewhere += jnp.where((target != z) | (r != z), 1, 0)
    pl.semaphore_wait(barrier, 2 * (n - 1) + 1 + elsewhere)

    right = lax.rem(z + 1, n)
    left = lax.rem(z + n - 1, n)

    def send(source, slot, chunk, plane):
        pltpu.make_async_remote_copy(
            src_ref=source,
            dst_ref=rows.at[slot, chunk],
            send_sem=ring_send,
            recv_sem=ring_recv.at[slot, chunk],
            device_id=at(r, plane),
            device_id_type=MESH,
        ).start()

    def arrived(slot, chunk):
        pltpu.make_async_copy(
            rows.at[slot, chunk], rows.at[slot, chunk], ring_recv.at[slot, chunk]
        ).wait()

    def ring_step(t):
        back = lax.rem(z - t + n, n)
        ahead = lax.rem(z + t, n)
        for slot, chunk, plane in (
            (back, 0, right),
            (ahead, 1, left),
            (back, 1, right),
            (ahead, 0, left),
        ):
            if t == half - 1 and chunk != (0 if plane is right else 1):
                if t > 0:
                    arrived(slot, chunk)
                continue
            if t == 0:
                send(g_ref.at[pl.ds(chunk * 128, 128)], slot, chunk, plane)
            else:
                arrived(slot, chunk)
                send(rows.at[slot, chunk], slot, chunk, plane)

    ring_step(0)

    for h in range(2):
        target = 2 * lax.rem(r, half) + h
        mine = (target == z) & (r == z)
        spot = cols.at[z // 2, lax.rem(z, 2), x_hi]

        @pl.when(mine)
        def _(h=h, spot=spot):
            pltpu.make_async_copy(g_ref.at[pl.ds(h * 128, 128)], spot, col_recv).start()

        @pl.when(jnp.logical_not(mine))
        def _(h=h, spot=spot, target=target):
            pltpu.make_async_remote_copy(
                src_ref=g_ref.at[pl.ds(h * 128, 128)],
                dst_ref=spot,
                send_sem=col_send.at[h],
                recv_sem=col_recv,
                device_id=at(z, target),
                device_id_type=MESH,
            ).start()

    gram = lax.dot_general(g_ref[...], g_ref[...], TN, preferred_element_type=F32)
    lane = lax.broadcasted_iota(jnp.int32, (BW, 128), 1)
    packed = jnp.concatenate(
        [
            jnp.where(
                lane < BW,
                gram[128 * m : 128 * m + BW, 128 * m : 128 * m + 128],
                gram[128 * m + BW : 128 * m + 128, 128 * m : 128 * m + 128],
            )
            for m in range(2)
        ],
        axis=0,
    )
    fsend[...] = packed.reshape(n, depth, 128)

    def scatter(d, _):
        to = lax.rem(r + d, n)
        pltpu.make_async_remote_copy(
            src_ref=fsend.at[to],
            dst_ref=frecv.at[r],
            send_sem=rs_send,
            recv_sem=rs_recv,
            device_id=at(to, z),
            device_id_type=MESH,
        ).start()
        return 0

    lax.fori_loop(1, n, scatter, 0)
    frecv[r] = fsend[r]
    rows[z] = g_ref[...].reshape(2, 128, 256)

    def drain(ref, sem):
        pltpu.make_async_copy(ref, ref, sem).wait()

    drain(frecv.at[pl.ds(0, n - 1)], rs_recv)
    total = frecv[0]
    for i in range(1, n):
        total = total + frecv[i]
    full[r] = total

    def share(d, _):
        pltpu.make_async_remote_copy(
            src_ref=full.at[r],
            dst_ref=full.at[r],
            send_sem=ag_send,
            recv_sem=ag_recv,
            device_id=at(lax.rem(r + d, n), z),
            device_id_type=MESH,
        ).start()
        return 0

    lax.fori_loop(1, n, share, 0)

    def maybe_ring(t):
        if t < half:
            ring_step(t)

    maybe_ring(1)

    drain(cols.at[pair, core], col_recv)

    def relay(d, _):
        pltpu.make_async_remote_copy(
            src_ref=cols.at[pair, core],
            dst_ref=cols.at[pair, core],
            send_sem=colg_send,
            recv_sem=colg_recv,
            device_id=at(lax.rem(r + 2 * d, n), z),
            device_id_type=MESH,
        ).start()
        return 0

    lax.fori_loop(1, half, relay, 0)

    drain(full.at[pl.ds(0, n - 1)], ag_recv)
    line = lax.broadcasted_iota(jnp.int32, (128, 128), 0)
    across = lax.broadcasted_iota(jnp.int32, (128, 128), 1)
    unit = (lax.rem(line, BW) == lax.rem(across, BW)).astype(F32)
    fisher = full[...].reshape(128, 128) * (1.0 / (n * 256)) + 0.1 * unit

    def split(array):
        array = array.reshape(2, 8, 8, 128)
        return jnp.stack([array[:, i] for i in range(8)], axis=0)

    def block_step(b, carry):
        blocks, inverse = eliminate(*carry, b)
        blocks = pltpu.roll(blocks.reshape(128, 128), 120, 1).reshape(8, 2, 8, 128)
        return rotate(blocks), rotate(inverse)

    maybe_ring(2)
    carry = lax.fori_loop(0, 4, block_step, (split(fisher), split(unit)))
    maybe_ring(3)
    _, inverse = lax.fori_loop(4, 8, block_step, carry)
    whole = jnp.concatenate([inverse[i, m] for m in range(2) for i in range(8)], axis=0)
    linv[...] = whole.reshape(n, depth, 128)

    inv[pair, core, z] = linv[r]

    def spread(d, _):
        pltpu.make_async_remote_copy(
            src_ref=linv.at[r],
            dst_ref=inv.at[pair, core, z],
            send_sem=ze_send,
            recv_sem=ze_recv,
            device_id=at(r, lax.rem(z + d, n)),
            device_id_type=MESH,
        ).start()
        return 0

    lax.fori_loop(1, n, spread, 0)

    other = at(r + 1 - 2 * core, z)

    def swap(buffer, send_sem, recv_sem):
        pltpu.make_async_remote_copy(
            src_ref=buffer.at[:, core],
            dst_ref=buffer.at[:, core],
            send_sem=send_sem,
            recv_sem=recv_sem,
            device_id=other,
            device_id_type=MESH,
        ).start()

    if half > 1:
        drain(cols.at[pl.ds(0, half - 1), 0], colg_recv)
    swap(cols, colx_send, colx_recv)
    maybe_ring(4)

    drain(inv.at[0, 0, pl.ds(0, n - 1)], ze_recv)

    def deal(d, _):
        pltpu.make_async_remote_copy(
            src_ref=inv.at[pair, core],
            dst_ref=inv.at[pair, core],
            send_sem=ig_send,
            recv_sem=ig_recv,
            device_id=at(lax.rem(r + 2 * d, n), z),
            device_id_type=MESH,
        ).start()
        return 0

    lax.fori_loop(1, half, deal, 0)
    maybe_ring(5)
    if half > 1:
        drain(inv.at[pl.ds(0, half - 1), 0], ig_recv)
    swap(inv, ix_send, ix_recv)
    maybe_ring(6)
    maybe_ring(7)
    drain(cols.at[:, 0], colx_recv)
    drain(inv.at[:, 0], ix_recv)
    far = lax.rem(z + half, n)
    arrived(far, 0)
    arrived(far, 1)

    part[...] = jnp.zeros_like(part)

    def plane_step(k, _):
        lower = inv[:, :, k].reshape(2, BW, 128)
        left_side = rows[k].reshape(256, 256)
        right_side = cols[k // 2, lax.rem(k, 2)].reshape(256, 256)
        for m in range(2):
            zero = jnp.zeros((BW, 128), F32)
            matrix = jnp.concatenate(
                [jnp.where(lane < BW, lower[m], zero), jnp.where(lane < BW, zero, lower[m])], axis=0
            )
            high = matrix.astype(BF16)
            rest = (matrix - high.astype(F32)).astype(BF16)

            def whiten(values):
                values = values[:, 128 * m : 128 * m + 128]
                return (
                    lax.dot_general(values, high, NT, preferred_element_type=F32)
                    + lax.dot_general(values, rest, NT, preferred_element_type=F32)
                ).astype(BF16)

            product = lax.dot_general(
                whiten(left_side), whiten(right_side), NT, preferred_element_type=F32
            )
            part[0] += product[:, :128]
            part[1] += product[:, 128:]
        return 0

    lax.fori_loop(0, n, plane_step, 0)

    give = pltpu.make_async_remote_copy(
        src_ref=part.at[1 - x_lo],
        dst_ref=precv,
        send_sem=p_send,
        recv_sem=p_recv,
        device_id={"row": r, "col": (1 - x_lo) * n + z},
        device_id_type=MESH,
    )
    give.start()

    drain(rows.at[pl.ds(0, n - 1)], ring_send)
    for h in range(2):
        target = 2 * lax.rem(r, half) + h

        @pl.when((target != z) | (r != z))
        def _(h=h):
            drain(rows.at[0, 0], col_send.at[h])

    drain(fsend.at[pl.ds(0, n - 1)], rs_send)
    drain(full.at[pl.ds(0, n - 1)], ag_send)
    drain(linv.at[pl.ds(0, n - 1)], ze_send)
    if half > 1:
        drain(cols.at[pl.ds(0, half - 1), 0], colg_send)
        drain(inv.at[pl.ds(0, half - 1), 0], ig_send)
    drain(cols.at[:, 0], colx_send)
    drain(inv.at[:, 0], ix_send)
    give.wait()
    out_ref[...] = (part[x_lo] + precv[...]) * (n * 512) ** (-0.5)


def solution(mesh):
    n = mesh.shape["row"]
    half = n // 2
    depth = 128 // n

    def per_device(grads):
        dma = pltpu.SemaphoreType.DMA
        return pl.pallas_call(
            functools.partial(kernel, n),
            out_shape=jax.ShapeDtypeStruct((256, 128), F32),
            in_specs=[pl.BlockSpec(memory_space=pltpu.VMEM)],
            out_specs=pl.BlockSpec(memory_space=pltpu.VMEM),
            scratch_shapes=[
                pltpu.VMEM((n, 2, 128, 256), BF16),
                pltpu.VMEM((half, 2, 2, 128, 256), BF16),
                pltpu.VMEM((n, depth, 128), F32),
                pltpu.VMEM((n, depth, 128), F32),
                pltpu.VMEM((n, depth, 128), F32),
                pltpu.VMEM((n, depth, 128), F32),
                pltpu.VMEM((half, 2, n, depth, 128), F32),
                pltpu.VMEM((2, 256, 128), F32),
                pltpu.VMEM((256, 128), F32),
                dma,
                dma((n, 2)),
                dma((2,)),
            ]
            + [dma] * 17,
            compiler_params=pltpu.CompilerParams(
                collective_id=0, has_side_effects=True, vmem_limit_bytes=40 * 2**20
            ),
        )(grads)

    return jax.shard_map(
        per_device,
        mesh=mesh,
        in_specs=(P("row", "col"),),
        out_specs=P("row", "col"),
        check_vma=False,
    )
```

```python
import functools

import jax
import jax.numpy as jnp
from jax import lax
from jax.experimental import pallas as pl
from jax.experimental.pallas import tpu as pltpu
from jax.sharding import PartitionSpec as P

BW = 64
F32 = jnp.float32
BF16 = jnp.bfloat16
MESH = pl.DeviceIdType.MESH
NT = (((1,), (1,)), ((), ()))
TN = (((0,), (0,)), ((), ()))


def eliminate(blocks, inverse):
    lane = lax.broadcasted_iota(jnp.int32, (1, 1, 8, 128), 3)
    sub = lax.broadcasted_iota(jnp.int32, (1, 1, 8, 128), 2)
    low = lane < BW
    for j in range(8):
        row = blocks[0:1, :, j : j + 1, :]
        other = inverse[0:1, :, j : j + 1, :]
        column = jnp.where(low, blocks[:, :, :, j : j + 1], blocks[:, :, :, BW + j : BW + j + 1])
        pivot = column[0:1, :, j : j + 1, :]
        first = jnp.where(sub > j, column[0:1], 0.0)
        column = jnp.concatenate([first, column[1:]], axis=0)
        inverted = 1.0 / pivot
        blocks = blocks - column * (row * inverted)
        inverse = inverse - column * (other * inverted)
        done = jnp.where(sub == j, inverse[0:1] * lax.rsqrt(pivot), inverse[0:1])
        inverse = jnp.concatenate([done, inverse[1:]], axis=0)
    return blocks, inverse


def kernel(
    n,
    g_ref,
    out_ref,
    rows,
    cols,
    fsend,
    frecv,
    full,
    linv,
    inv,
    part,
    precv,
    pre,
    wrow,
    wcol,
    ring_recv,
    col_send,
    p_send,
    p_recv,
    ring_send,
    pre_send,
    pre_recv,
    col_recv,
    colg_send,
    colg_recv,
    colx_send,
    colx_recv,
    rs_send,
    rs_recv,
    ag_send,
    ag_recv,
    ze_send,
    ze_recv,
    ig_send,
    ig_recv,
    ix_send,
    ix_recv,
):
    r = lax.axis_index("row")
    c = lax.axis_index("col")
    half = n // 2
    quad = half // 2
    x_lo = c // n
    z = lax.rem(c, n)
    x_hi = r // half
    q = lax.rem(r, half)
    y = q // 2
    pair = r // 2
    core = lax.rem(r, 2)
    depth = 128 // n

    def at(row, plane):
        return {"row": row, "col": x_lo * n + plane}

    across = {"row": r, "col": (1 - x_lo) * n + z}

    barrier = pltpu.get_barrier_semaphore()

    def greet(d, _):
        pl.semaphore_signal(barrier, 1, device_id=at(lax.rem(r + d, n), z), device_id_type=MESH)
        pl.semaphore_signal(barrier, 1, device_id=at(r, lax.rem(z + d, n)), device_id_type=MESH)
        return 0

    lax.fori_loop(1, n, greet, 0)
    pl.semaphore_signal(barrier, 1, device_id=across, device_id_type=MESH)
    pl.semaphore_wait(barrier, 2 * (n - 1) + 1)

    def push(source, target, send_sem, recv_sem, device):
        copy = pltpu.make_async_remote_copy(
            src_ref=source,
            dst_ref=target,
            send_sem=send_sem,
            recv_sem=recv_sem,
            device_id=device,
            device_id_type=MESH,
        )
        copy.start()
        return copy

    def drain(ref, sem):
        pltpu.make_async_copy(ref, ref, sem).wait()

    def keep_or_push(local, source, target, send_sem, recv_sem, device):
        @pl.when(local)
        def _():
            pltpu.make_async_copy(source, target, recv_sem).start()

        @pl.when(jnp.logical_not(local))
        def _():
            push(source, target, send_sem, recv_sem, device)

    right = lax.rem(z + 1, n)
    left = lax.rem(z + n - 1, n)

    def arrived(slot, chunk):
        drain(rows.at[slot, chunk], ring_recv.at[slot, chunk])

    def ring_step(t):
        if t >= half:
            return
        back = lax.rem(z - t + n, n)
        ahead = lax.rem(z + t, n)
        for slot, chunk, plane, last in (
            (back, 0, right, True),
            (ahead, 1, left, True),
            (back, 1, right, False),
            (ahead, 0, left, False),
        ):
            source = rows.at[slot, chunk]
            if t == 0:
                source = g_ref.at[pl.ds(chunk * 128, 128)]
            else:
                arrived(slot, chunk)
            if t < half - 1 or last:
                push(source, rows.at[slot, chunk], ring_send, ring_recv.at[slot, chunk], at(r, plane))

    ring_step(0)

    gram = lax.dot_general(g_ref[...], g_ref[...], TN, preferred_element_type=F32)
    lane = lax.broadcasted_iota(jnp.int32, (BW, 128), 1)
    packed = jnp.concatenate(
        [
            jnp.where(
                lane < BW,
                gram[128 * m : 128 * m + BW, 128 * m : 128 * m + 128],
                gram[128 * m + BW : 128 * m + 128, 128 * m : 128 * m + 128],
            )
            for m in range(2)
        ],
        axis=0,
    )
    fsend[...] = packed.reshape(n, depth, 128)

    def scatter(d, _):
        to = lax.rem(r + d, n)
        push(fsend.at[to], frecv.at[r], rs_send, rs_recv, at(to, z))
        return 0

    lax.fori_loop(1, n, scatter, 0)

    first = lax.rem(q - z // 2 + half, half)
    hop = x_hi * half + lax.rem(first, quad) * 2 + first // quad
    keep_or_push(hop == r, g_ref, pre, pre_send, pre_recv, at(hop, z))

    frecv[r] = fsend[r]
    rows[z] = g_ref[...].reshape(2, 128, 256)

    drain(frecv.at[pl.ds(0, n - 1)], rs_recv)
    total = frecv[0]
    for i in range(1, n):
        total = total + frecv[i]
    full[r] = total

    def share(d, _):
        push(full.at[r], full.at[r], ag_send, ag_recv, at(lax.rem(r + d, n), z))
        return 0

    lax.fori_loop(1, n, share, 0)

    drain(pre, pre_recv)
    here = 2 * lax.rem(core * quad + y + z // 2, half)
    spot = cols.at[x_hi, core, y]
    for h in range(2):
        keep_or_push(
            here + h == z,
            pre.at[pl.ds(128 * h, 128)],
            spot.at[lax.rem(z, 2)],
            col_send.at[h],
            col_recv,
            at(r, here + h),
        )

    ring_step(1)

    drain(full.at[pl.ds(0, n - 1)], ag_recv)
    line = lax.broadcasted_iota(jnp.int32, (128, 128), 0)
    place = lax.broadcasted_iota(jnp.int32, (128, 128), 1)
    unit = (lax.rem(line, BW) == lax.rem(place, BW)).astype(F32)
    fisher = full[...].reshape(128, 128) * (1.0 / (n * 256)) + 0.1 * unit

    def split(array):
        array = array.reshape(2, 8, 8, 128)
        return jnp.stack([array[:, i] for i in range(8)], axis=0)

    def block_step(b, carry):
        blocks, inverse = eliminate(*carry)
        blocks = pltpu.roll(blocks.reshape(128, 128), 120, 1).reshape(8, 2, 8, 128)
        return (
            jnp.concatenate([blocks[1:], jnp.zeros_like(blocks[:1])], axis=0),
            jnp.concatenate([inverse[1:], inverse[:1]], axis=0),
        )

    ring_step(2)
    carry = lax.fori_loop(0, 5, block_step, (split(fisher), split(unit)))
    ring_step(3)
    _, inverse = lax.fori_loop(5, 8, block_step, carry)
    whole = jnp.concatenate([inverse[i, m] for m in range(2) for i in range(8)], axis=0)
    linv[...] = whole.reshape(n, depth, 128)

    inv[pair, core, z] = linv[r]

    def spread(d, _):
        push(linv.at[r], inv.at[pair, core, z], ze_send, ze_recv, at(r, lax.rem(z + d, n)))
        return 0

    lax.fori_loop(1, n, spread, 0)

    drain(spot, col_recv)

    def relay(d, _):
        push(spot, spot, colg_send, colg_recv, at(lax.rem(r + 2 * d, n), z))
        return 0

    lax.fori_loop(1, half, relay, 0)
    ring_step(4)

    drain(inv.at[0, 0, pl.ds(0, n - 1)], ze_recv)

    def deal(d, _):
        mine = inv.at[pair, core]
        push(mine, mine, ig_send, ig_recv, at(lax.rem(r + 2 * d, n), z))
        return 0

    lax.fori_loop(1, half, deal, 0)

    other = at(r + 1 - 2 * core, z)
    ring_step(5)
    drain(rows.at[pl.ds(0, half - 1)], colg_recv)
    push(cols.at[:, core], cols.at[:, core], colx_send, colx_recv, other)
    drain(inv.at[pl.ds(0, half - 1), 0], ig_recv)
    push(inv.at[:, core], inv.at[:, core], ix_send, ix_recv, other)
    ring_step(6)
    ring_step(7)
    drain(cols.at[:, 0], colx_recv)
    drain(inv.at[:, 0], ix_recv)

    wide = lax.broadcasted_iota(jnp.int32, (BW, 256), 1)

    def whiten_plane(k):
        lower = inv[:, :, k].reshape(2, BW, 128)
        zero = jnp.zeros((BW, 128), F32)
        both = [
            jnp.concatenate([lower[0], zero], axis=1),
            jnp.concatenate([zero, lower[1]], axis=1),
        ]
        matrix = jnp.concatenate(
            [jnp.where(wide // BW == i, both[i // 2], 0.0) for i in range(4)], axis=0
        )
        high = matrix.astype(BF16)
        rest = (matrix - high.astype(F32)).astype(BF16)
        offset = pl.ds(pl.multiple_of(k * 256, 256), 256)
        slot = lax.rem(z // 2 - k // 2 + half, half)

        def whiten(values):
            return (
                lax.dot_general(values, high, NT, preferred_element_type=F32)
                + lax.dot_general(values, rest, NT, preferred_element_type=F32)
            ).astype(BF16)

        wrow[:, offset] = whiten(rows[k].reshape(256, 256))
        for i in range(2):
            values = cols[i, slot // quad, lax.rem(slot, quad), lax.rem(k, 2)]
            wcol[128 * i : 128 * i + 128, offset] = whiten(values)

    def plane_step(d, _):
        whiten_plane(lax.rem(z + half + 1 + d, n))
        return 0

    lax.fori_loop(0, n - 1, plane_step, 0)
    far = lax.rem(z + half, n)
    arrived(far, 0)
    arrived(far, 1)
    whiten_plane(far)

    gives = []
    for i in range(2):
        product = lax.dot_general(
            wrow[128 * i : 128 * i + 128, :], wcol[...], NT, preferred_element_type=F32
        )
        part[0, i] = product[:, :128]
        part[1, i] = product[:, 128:]
        gives.append(
            push(part.at[1 - x_lo, i], precv.at[i], p_send.at[i], p_recv.at[i], across)
        )

    drain(rows.at[pl.ds(0, n - 1)], ring_send)

    @pl.when(hop != r)
    def _():
        drain(pre, pre_send)

    for h in range(2):

        @pl.when(here + h != z)
        def _(h=h):
            drain(rows.at[0, 0], col_send.at[h])

    drain(fsend.at[pl.ds(0, n - 1)], rs_send)
    drain(full.at[pl.ds(0, n - 1)], ag_send)
    drain(linv.at[pl.ds(0, n - 1)], ze_send)
    drain(rows.at[pl.ds(0, half - 1)], colg_send)
    drain(inv.at[pl.ds(0, half - 1), 0], ig_send)
    drain(cols.at[:, 0], colx_send)
    drain(inv.at[:, 0], ix_send)
    for i in range(2):
        gives[i].wait()
        out_ref[128 * i : 128 * i + 128, :] = (part[x_lo, i] + precv[i]) * (n * 512) ** (-0.5)


def solution(mesh):
    n = mesh.shape["row"]
    half = n // 2
    depth = 128 // n

    def per_device(grads):
        dma = pltpu.SemaphoreType.DMA
        return pl.pallas_call(
            functools.partial(kernel, n),
            out_shape=jax.ShapeDtypeStruct((256, 128), F32),
            in_specs=[pl.BlockSpec(memory_space=pltpu.VMEM)],
            out_specs=pl.BlockSpec(memory_space=pltpu.VMEM),
            scratch_shapes=[
                pltpu.VMEM((n, 2, 128, 256), BF16),
                pltpu.VMEM((2, 2, half // 2, 2, 128, 256), BF16),
                pltpu.VMEM((n, depth, 128), F32),
                pltpu.VMEM((n, depth, 128), F32),
                pltpu.VMEM((n, depth, 128), F32),
                pltpu.VMEM((n, depth, 128), F32),
                pltpu.VMEM((half, 2, n, depth, 128), F32),
                pltpu.VMEM((2, 2, 128, 128), F32),
                pltpu.VMEM((2, 128, 128), F32),
                pltpu.VMEM((256, 256), BF16),
                pltpu.VMEM((256, n * 256), BF16),
                pltpu.VMEM((256, n * 256), BF16),
                dma((n, 2)),
                dma((2,)),
                dma((2,)),
                dma((2,)),
            ]
            + [dma] * 18,
            compiler_params=pltpu.CompilerParams(
                collective_id=0, has_side_effects=True, vmem_limit_bytes=40 * 2**20
            ),
        )(grads)

    return jax.shard_map(
        per_device,
        mesh=mesh,
        in_specs=(P("row", "col"),),
        out_specs=P("row", "col"),
        check_vma=False,
    )
```

```python
import functools

import jax
import jax.numpy as jnp
from jax import lax
from jax.experimental import pallas as pl
from jax.experimental.pallas import tpu as pltpu
from jax.sharding import PartitionSpec as P

BW = 64
CHUNKS = 4
SIZE = 256 // CHUNKS
F32 = jnp.float32
BF16 = jnp.bfloat16
MESH = pl.DeviceIdType.MESH
NT = (((1,), (1,)), ((), ()))
TN = (((0,), (0,)), ((), ()))


def eliminate(blocks, inverse):
    lane = lax.broadcasted_iota(jnp.int32, (1, 1, 8, 128), 3)
    sub = lax.broadcasted_iota(jnp.int32, (1, 1, 8, 128), 2)
    low = lane < BW
    for start in (0, 4):
        four = range(start, start + 4)
        columns = [
            jnp.where(low, blocks[:, :, :, j : j + 1], blocks[:, :, :, BW + j : BW + j + 1])
            for j in four
        ]
        factor = [[None] * 4 for _ in range(4)]
        root = [None] * 4
        for v in range(4):
            for u in range(v, 4):
                entry = columns[v][0:1, :, start + u : start + u + 1, :]
                for w in range(v):
                    entry = entry - factor[u][w] * factor[v][w]
                if u == v:
                    root[v] = lax.rsqrt(entry)
                else:
                    factor[u][v] = entry * root[v]

        def solve(array):
            forward = []
            for u in range(4):
                row = array[0:1, :, start + u : start + u + 1, :]
                for w in range(u):
                    row = row - factor[u][w] * forward[w]
                forward.append(row * root[u])
            back = [None] * 4
            for u in reversed(range(4)):
                row = forward[u]
                for w in range(u + 1, 4):
                    row = row - factor[w][u] * back[w]
                back[u] = row * root[u]
            return forward, back

        _, take = solve(blocks)
        done, other = solve(inverse)
        columns = [
            jnp.concatenate([jnp.where(sub > start + 3, column[0:1], 0.0), column[1:]], axis=0)
            for column in columns
        ]
        for v in range(4):
            blocks = blocks - columns[v] * take[v]
            inverse = inverse - columns[v] * other[v]
        top = inverse[0:1]
        for u in range(4):
            top = jnp.where(sub == start + u, done[u], top)
        inverse = jnp.concatenate([top, inverse[1:]], axis=0)
    return blocks, inverse


def kernel(
    n,
    g_ref,
    out_ref,
    rows,
    cols,
    fsend,
    frecv,
    full,
    linv,
    inv,
    part,
    precv,
    pre,
    wrow,
    wcol,
    ring_recv,
    col_send,
    p_send,
    p_recv,
    ring_send,
    pre_send,
    pre_recv,
    col_recv,
    colg_send,
    colg_recv,
    colx_send,
    colx_recv,
    rs_send,
    rs_recv,
    ag_send,
    ag_recv,
    ze_send,
    ze_recv,
    ig_send,
    ig_recv,
    ix_send,
    ix_recv,
):
    r = lax.axis_index("row")
    c = lax.axis_index("col")
    half = n // 2
    quad = half // 2
    x_lo = c // n
    z = lax.rem(c, n)
    x_hi = r // half
    q = lax.rem(r, half)
    y = q // 2
    pair = r // 2
    core = lax.rem(r, 2)
    depth = 128 // n

    def at(row, plane):
        return {"row": row, "col": x_lo * n + plane}

    across = {"row": r, "col": (1 - x_lo) * n + z}

    barrier = pltpu.get_barrier_semaphore()

    def greet(d, _):
        pl.semaphore_signal(barrier, 1, device_id=at(lax.rem(r + d, n), z), device_id_type=MESH)
        pl.semaphore_signal(barrier, 1, device_id=at(r, lax.rem(z + d, n)), device_id_type=MESH)
        return 0

    lax.fori_loop(1, n, greet, 0)
    pl.semaphore_signal(barrier, 1, device_id=across, device_id_type=MESH)
    pl.semaphore_wait(barrier, 2 * (n - 1) + 1)

    def push(source, target, send_sem, recv_sem, device):
        copy = pltpu.make_async_remote_copy(
            src_ref=source,
            dst_ref=target,
            send_sem=send_sem,
            recv_sem=recv_sem,
            device_id=device,
            device_id_type=MESH,
        )
        copy.start()
        return copy

    def drain(ref, sem):
        pltpu.make_async_copy(ref, ref, sem).wait()

    def keep_or_push(local, source, target, send_sem, recv_sem, device):
        @pl.when(local)
        def _():
            pltpu.make_async_copy(source, target, recv_sem).start()

        @pl.when(jnp.logical_not(local))
        def _():
            push(source, target, send_sem, recv_sem, device)

    right = lax.rem(z + 1, n)
    left = lax.rem(z + n - 1, n)

    def arrived(slot, chunk):
        drain(rows.at[slot, chunk], ring_recv.at[slot, chunk])

    def ring_step(t):
        if t >= half:
            return
        back = lax.rem(z - t + n, n)
        ahead = lax.rem(z + t, n)
        for i in range(CHUNKS):
            for slot, chunk, plane in ((back, i, right), (ahead, CHUNKS - 1 - i, left)):
                source = rows.at[slot, chunk]
                if t == 0:
                    source = g_ref.at[pl.ds(chunk * SIZE, SIZE)]
                else:
                    arrived(slot, chunk)
                if t < half - 1 or i < CHUNKS // 2:
                    push(
                        source,
                        rows.at[slot, chunk],
                        ring_send,
                        ring_recv.at[slot, chunk],
                        at(r, plane),
                    )

    lane = lax.broadcasted_iota(jnp.int32, (BW, 128), 1)
    line = lax.broadcasted_iota(jnp.int32, (128, 128), 0)
    place = lax.broadcasted_iota(jnp.int32, (128, 128), 1)
    unit = (lax.rem(line, BW) == lax.rem(place, BW)).astype(F32)
    other = at(r + 1 - 2 * core, z)

    def fisher_scatter():
        gram = lax.dot_general(g_ref[...], g_ref[...], TN, preferred_element_type=F32)
        packed = jnp.concatenate(
            [
                jnp.where(
                    lane < BW,
                    gram[128 * m : 128 * m + BW, 128 * m : 128 * m + 128],
                    gram[128 * m + BW : 128 * m + 128, 128 * m : 128 * m + 128],
                )
                for m in range(2)
            ],
            axis=0,
        )
        fsend[...] = packed.reshape(n, depth, 128)

        def scatter(d, _):
            to = lax.rem(r + d, n)
            push(fsend.at[to], frecv.at[r], rs_send, rs_recv, at(to, z))
            return 0

        lax.fori_loop(1, n, scatter, 0)
        frecv[r] = fsend[r]

    first = lax.rem(q - z // 2 + half, half)
    hop = x_hi * half + lax.rem(first, quad) * 2 + first // quad

    def columns_hop():
        keep_or_push(hop == r, g_ref, pre, pre_send, pre_recv, at(hop, z))
        rows[z] = g_ref[...].reshape(CHUNKS, SIZE, 256)

    def fisher_share():
        drain(frecv.at[pl.ds(0, n - 1)], rs_recv)
        total = frecv[0]
        for i in range(1, n):
            total = total + frecv[i]
        full[r] = total

        def share(d, _):
            push(full.at[r], full.at[r], ag_send, ag_recv, at(lax.rem(r + d, n), z))
            return 0

        lax.fori_loop(1, n, share, 0)

    here = 2 * lax.rem(core * quad + y + z // 2, half)
    spot = cols.at[x_hi, core, y]

    def columns_along():
        drain(pre, pre_recv)
        for h in range(2):
            keep_or_push(
                here + h == z,
                pre.at[pl.ds(128 * h, 128)],
                spot.at[lax.rem(z, 2)],
                col_send.at[h],
                col_recv,
                at(r, here + h),
            )

    def fisher_matrix():
        drain(full.at[pl.ds(0, n - 1)], ag_recv)
        fisher = full[...].reshape(128, 128) * (1.0 / (n * 256)) + 0.1 * unit
        return split(fisher), split(unit)

    def split(array):
        array = array.reshape(2, 8, 8, 128)
        return jnp.stack([array[:, i] for i in range(8)], axis=0)

    def block_step(b, carry):
        blocks, inverse = eliminate(*carry)
        blocks = pltpu.roll(blocks.reshape(128, 128), 120, 1).reshape(8, 2, 8, 128)
        return (
            jnp.concatenate([blocks[1:], jnp.zeros_like(blocks[:1])], axis=0),
            jnp.concatenate([inverse[1:], inverse[:1]], axis=0),
        )

    def inverse_along(inverse):
        whole = jnp.concatenate([inverse[i, m] for m in range(2) for i in range(8)], axis=0)
        linv[...] = whole.reshape(n, depth, 128)
        inv[pair, core, z] = linv[r]

        def spread(d, _):
            push(linv.at[r], inv.at[pair, core, z], ze_send, ze_recv, at(r, lax.rem(z + d, n)))
            return 0

        lax.fori_loop(1, n, spread, 0)

    def columns_gather():
        drain(spot, col_recv)

        def relay(d, _):
            push(spot, spot, colg_send, colg_recv, at(lax.rem(r + 2 * d, n), z))
            return 0

        lax.fori_loop(1, half, relay, 0)

    def inverse_gather():
        drain(inv.at[0, 0, pl.ds(0, n - 1)], ze_recv)

        def deal(d, _):
            mine = inv.at[pair, core]
            push(mine, mine, ig_send, ig_recv, at(lax.rem(r + 2 * d, n), z))
            return 0

        lax.fori_loop(1, half, deal, 0)

    def columns_swap():
        drain(rows.at[pl.ds(0, half - 1)], colg_recv)
        push(cols.at[:, core], cols.at[:, core], colx_send, colx_recv, other)

    def inverse_swap():
        drain(inv.at[pl.ds(0, half - 1), 0], ig_recv)
        push(inv.at[:, core], inv.at[:, core], ix_send, ix_recv, other)

    columns_hop()
    ring_step(0)
    fisher_scatter()
    columns_along()
    ring_step(1)
    fisher_share()
    carry = fisher_matrix()
    ring_step(2)
    carry = lax.fori_loop(0, 4, block_step, carry)
    columns_gather()
    carry = lax.fori_loop(4, 8, block_step, carry)
    inverse_along(carry[1])
    ring_step(3)
    ring_step(4)
    inverse_gather()
    ring_step(5)
    ring_step(6)
    inverse_swap()
    ring_step(7)
    columns_swap()
    drain(inv.at[:, 0], ix_recv)
    drain(cols.at[:, 0], colx_recv)

    wide = lax.broadcasted_iota(jnp.int32, (BW, 256), 1)

    def whiten_plane(k):
        lower = inv[:, :, k].reshape(2, BW, 128)
        zero = jnp.zeros((BW, 128), F32)
        both = [
            jnp.concatenate([lower[0], zero], axis=1),
            jnp.concatenate([zero, lower[1]], axis=1),
        ]
        matrix = jnp.concatenate(
            [jnp.where(wide // BW == i, both[i // 2], 0.0) for i in range(4)], axis=0
        )
        high = matrix.astype(BF16)
        rest = (matrix - high.astype(F32)).astype(BF16)
        offset = pl.ds(pl.multiple_of(k * 256, 256), 256)
        slot = lax.rem(z // 2 - k // 2 + half, half)

        where = (slot // quad, lax.rem(slot, quad), lax.rem(k, 2))
        values = jnp.concatenate(
            [rows[k].reshape(256, 256), cols[(0, *where)], cols[(1, *where)]], axis=0
        )
        white = lax.dot_general(
            jnp.concatenate([values, values], axis=1),
            jnp.concatenate([high, rest], axis=1),
            NT,
            preferred_element_type=F32,
        ).astype(BF16)
        wrow[:, offset] = white[:256]
        wcol[0, :, offset] = white[256:384]
        wcol[1, :, offset] = white[384:]

    def plane_step(d, _):
        whiten_plane(lax.rem(z + half + 1 + d, n))
        return 0

    lax.fori_loop(0, n - 1, plane_step, 0, unroll=3)
    far = lax.rem(z + half, n)
    for i in range(CHUNKS):
        arrived(far, i)
    whiten_plane(far)

    def product(i):
        return lax.dot_general(wrow[...], wcol[i], NT, preferred_element_type=F32)

    part[...] = product(1 - x_lo)
    give = push(part, precv, p_send, p_recv, across)
    own = product(x_lo)

    drain(rows.at[pl.ds(0, n - 1)], ring_send)

    @pl.when(hop != r)
    def _():
        drain(pre, pre_send)

    for h in range(2):

        @pl.when(here + h != z)
        def _(h=h):
            drain(cols.at[0, 0, 0, 0], col_send.at[h])

    drain(fsend.at[pl.ds(0, n - 1)], rs_send)
    drain(full.at[pl.ds(0, n - 1)], ag_send)
    drain(linv.at[pl.ds(0, n - 1)], ze_send)
    drain(rows.at[pl.ds(0, half - 1)], colg_send)
    drain(inv.at[pl.ds(0, half - 1), 0], ig_send)
    drain(cols.at[:, 0], colx_send)
    drain(inv.at[:, 0], ix_send)
    give.wait()
    out_ref[...] = (own + precv[...]) * (n * 512) ** (-0.5)


def solution(mesh):
    n = mesh.shape["row"]
    half = n // 2
    depth = 128 // n

    def per_device(grads):
        dma = pltpu.SemaphoreType.DMA
        return pl.pallas_call(
            functools.partial(kernel, n),
            out_shape=jax.ShapeDtypeStruct((256, 128), F32),
            in_specs=[pl.BlockSpec(memory_space=pltpu.VMEM)],
            out_specs=pl.BlockSpec(memory_space=pltpu.VMEM),
            scratch_shapes=[
                pltpu.VMEM((n, CHUNKS, SIZE, 256), BF16),
                pltpu.VMEM((2, 2, half // 2, 2, 128, 256), BF16),
                pltpu.VMEM((n, depth, 128), F32),
                pltpu.VMEM((n, depth, 128), F32),
                pltpu.VMEM((n, depth, 128), F32),
                pltpu.VMEM((n, depth, 128), F32),
                pltpu.VMEM((half, 2, n, depth, 128), F32),
                pltpu.VMEM((256, 128), F32),
                pltpu.VMEM((256, 128), F32),
                pltpu.VMEM((256, 256), BF16),
                pltpu.VMEM((256, n * 256), BF16),
                pltpu.VMEM((2, 128, n * 256), BF16),
                dma((n, CHUNKS)),
                dma((2,)),
            ]
            + [dma] * 20,
            compiler_params=pltpu.CompilerParams(
                collective_id=0, has_side_effects=True, vmem_limit_bytes=40 * 2**20
            ),
        )(grads)

    return jax.shard_map(
        per_device,
        mesh=mesh,
        in_specs=(P("row", "col"),),
        out_specs=P("row", "col"),
        check_vma=False,
    )
```

```python
import functools

import jax
import jax.numpy as jnp
from jax import lax
from jax.experimental import pallas as pl
from jax.experimental.pallas import tpu as pltpu
from jax.sharding import PartitionSpec as P

BW = 64
CHUNKS = 4
SIZE = 256 // CHUNKS
F32 = jnp.float32
BF16 = jnp.bfloat16
MESH = pl.DeviceIdType.MESH
NT = (((1,), (1,)), ((), ()))
TN = (((0,), (0,)), ((), ()))


def eliminate(blocks, inverse):
    lane = lax.broadcasted_iota(jnp.int32, (1, 1, 8, 128), 3)
    sub = lax.broadcasted_iota(jnp.int32, (1, 1, 8, 128), 2)
    low = lane < BW
    for start in (0, 4):
        four = range(start, start + 4)
        columns = [
            jnp.where(low, blocks[:, :, :, j : j + 1], blocks[:, :, :, BW + j : BW + j + 1])
            for j in four
        ]
        factor = [[None] * 4 for _ in range(4)]
        root = [None] * 4
        for v in range(4):
            for u in range(v, 4):
                entry = columns[v][0:1, :, start + u : start + u + 1, :]
                for w in range(v):
                    entry = entry - factor[u][w] * factor[v][w]
                if u == v:
                    root[v] = lax.rsqrt(entry)
                else:
                    factor[u][v] = entry * root[v]

        def solve(array):
            forward = []
            for u in range(4):
                row = array[0:1, :, start + u : start + u + 1, :]
                for w in range(u):
                    row = row - factor[u][w] * forward[w]
                forward.append(row * root[u])
            back = [None] * 4
            for u in reversed(range(4)):
                row = forward[u]
                for w in range(u + 1, 4):
                    row = row - factor[w][u] * back[w]
                back[u] = row * root[u]
            return forward, back

        _, take = solve(blocks)
        done, other = solve(inverse)
        columns = [
            jnp.concatenate([jnp.where(sub > start + 3, column[0:1], 0.0), column[1:]], axis=0)
            for column in columns
        ]
        for v in range(4):
            blocks = blocks - columns[v] * take[v]
            inverse = inverse - columns[v] * other[v]
        top = inverse[0:1]
        for u in range(4):
            top = jnp.where(sub == start + u, done[u], top)
        inverse = jnp.concatenate([top, inverse[1:]], axis=0)
    return blocks, inverse


def kernel(
    n,
    g_ref,
    out_ref,
    rows,
    cols,
    fsend,
    frecv,
    full,
    linv,
    inv,
    part,
    precv,
    pre,
    wrow,
    wcol,
    ring_recv,
    col_send,
    p_send,
    p_recv,
    ring_send,
    pre_send,
    pre_recv,
    col_recv,
    colg_send,
    colg_recv,
    colx_send,
    colx_recv,
    rs_send,
    rs_recv,
    ag_send,
    ag_recv,
    ze_send,
    ze_recv,
    ig_send,
    ig_recv,
    ix_send,
    ix_recv,
):
    r = lax.axis_index("row")
    c = lax.axis_index("col")
    half = n // 2
    quad = half // 2
    x_lo = c // n
    z = lax.rem(c, n)
    x_hi = r // half
    q = lax.rem(r, half)
    y = q // 2
    pair = r // 2
    core = lax.rem(r, 2)
    depth = 128 // n

    def at(row, plane):
        return {"row": row, "col": x_lo * n + plane}

    across = {"row": r, "col": (1 - x_lo) * n + z}

    barrier = pltpu.get_barrier_semaphore()

    def greet(d, _):
        pl.semaphore_signal(barrier, 1, device_id=at(lax.rem(r + d, n), z), device_id_type=MESH)
        pl.semaphore_signal(barrier, 1, device_id=at(r, lax.rem(z + d, n)), device_id_type=MESH)
        return 0

    lax.fori_loop(1, n, greet, 0)
    pl.semaphore_signal(barrier, 1, device_id=across, device_id_type=MESH)
    pl.semaphore_wait(barrier, 2 * (n - 1) + 1)

    def push(source, target, send_sem, recv_sem, device):
        copy = pltpu.make_async_remote_copy(
            src_ref=source,
            dst_ref=target,
            send_sem=send_sem,
            recv_sem=recv_sem,
            device_id=device,
            device_id_type=MESH,
        )
        copy.start()
        return copy

    def drain(ref, sem):
        pltpu.make_async_copy(ref, ref, sem).wait()

    def keep_or_push(local, source, target, send_sem, recv_sem, device):
        @pl.when(local)
        def _():
            pltpu.make_async_copy(source, target, recv_sem).start()

        @pl.when(jnp.logical_not(local))
        def _():
            push(source, target, send_sem, recv_sem, device)

    right = lax.rem(z + 1, n)
    left = lax.rem(z + n - 1, n)

    def arrived(slot, chunk):
        drain(rows.at[slot, chunk], ring_recv.at[slot, chunk])

    def ring_step(t):
        if t >= half:
            return
        back = lax.rem(z - t + n, n)
        ahead = lax.rem(z + t, n)
        for i in range(CHUNKS):
            for slot, chunk, plane in ((back, i, right), (ahead, CHUNKS - 1 - i, left)):
                source = rows.at[slot, chunk]
                if t == 0:
                    source = g_ref.at[pl.ds(chunk * SIZE, SIZE)]
                else:
                    arrived(slot, chunk)
                if t < half - 1 or i < CHUNKS // 2:
                    push(
                        source,
                        rows.at[slot, chunk],
                        ring_send,
                        ring_recv.at[slot, chunk],
                        at(r, plane),
                    )

    lane = lax.broadcasted_iota(jnp.int32, (BW, 128), 1)
    line = lax.broadcasted_iota(jnp.int32, (128, 128), 0)
    place = lax.broadcasted_iota(jnp.int32, (128, 128), 1)
    unit = (lax.rem(line, BW) == lax.rem(place, BW)).astype(F32)
    other = at(r + 1 - 2 * core, z)

    def fisher_scatter():
        gram = lax.dot_general(g_ref[...], g_ref[...], TN, preferred_element_type=F32)
        packed = jnp.concatenate(
            [
                jnp.where(
                    lane < BW,
                    gram[128 * m : 128 * m + BW, 128 * m : 128 * m + 128],
                    gram[128 * m + BW : 128 * m + 128, 128 * m : 128 * m + 128],
                )
                for m in range(2)
            ],
            axis=0,
        )
        fsend[...] = packed.reshape(n, depth, 128)

        def scatter(d, _):
            to = lax.rem(r + d, n)
            push(fsend.at[to], frecv.at[r], rs_send, rs_recv, at(to, z))
            return 0

        lax.fori_loop(1, n, scatter, 0)
        frecv[r] = fsend[r]

    def spot_of(m):
        if quad == 1:
            return m, 0
        return lax.rem(m // 2, 2), m // 4 * 2 + lax.rem(m, 2)

    hop_core, hop_y = spot_of(lax.rem(q + 3 * (z // 2), half))
    hop = x_hi * half + hop_y * 2 + hop_core
    me = core if quad == 1 else y // 2 * 4 + core * 2 + lax.rem(y, 2)

    def columns_hop():
        keep_or_push(hop == r, g_ref, pre, pre_send, pre_recv, at(hop, z))
        rows[z] = g_ref[...].reshape(CHUNKS, SIZE, 256)

    def fisher_share():
        drain(frecv.at[pl.ds(0, n - 1)], rs_recv)
        total = frecv[0]
        for i in range(1, n):
            total = total + frecv[i]
        full[r] = total

        def share(d, _):
            push(full.at[r], full.at[r], ag_send, ag_recv, at(lax.rem(r + d, n), z))
            return 0

        lax.fori_loop(1, n, share, 0)

    here = 2 * lax.rem(me + (4 * half - 3) * (z // 2), half)
    spot = cols.at[x_hi, core, y]

    def columns_along():
        drain(pre, pre_recv)
        for h in range(2):
            keep_or_push(
                here + h == z,
                pre.at[pl.ds(128 * h, 128)],
                spot.at[lax.rem(z, 2)],
                col_send.at[h],
                col_recv,
                at(r, here + h),
            )

    def fisher_matrix():
        drain(full.at[pl.ds(0, n - 1)], ag_recv)
        fisher = full[...].reshape(128, 128) * (1.0 / (n * 256)) + 0.1 * unit
        return split(fisher), split(unit)

    def split(array):
        array = array.reshape(2, 8, 8, 128)
        return jnp.stack([array[:, i] for i in range(8)], axis=0)

    def block_step(b, carry):
        blocks, inverse = eliminate(*carry)
        blocks = pltpu.roll(blocks.reshape(128, 128), 120, 1).reshape(8, 2, 8, 128)
        return (
            jnp.concatenate([blocks[1:], jnp.zeros_like(blocks[:1])], axis=0),
            jnp.concatenate([inverse[1:], inverse[:1]], axis=0),
        )

    def inverse_along(inverse):
        whole = jnp.concatenate([inverse[i, m] for m in range(2) for i in range(8)], axis=0)
        linv[...] = whole.reshape(n, depth, 128)
        inv[pair, core, z] = linv[r]

        def spread(d, _):
            push(linv.at[r], inv.at[pair, core, z], ze_send, ze_recv, at(r, lax.rem(z + d, n)))
            return 0

        lax.fori_loop(1, n, spread, 0)

    def columns_gather():
        drain(spot, col_recv)

        def relay(d, _):
            push(spot, spot, colg_send, colg_recv, at(lax.rem(r + 2 * d, n), z))
            return 0

        lax.fori_loop(1, half, relay, 0)

    def inverse_gather():
        drain(inv.at[0, 0, pl.ds(0, n - 1)], ze_recv)

        def deal(d, _):
            mine = inv.at[pair, core]
            push(mine, mine, ig_send, ig_recv, at(lax.rem(r + 2 * d, n), z))
            return 0

        lax.fori_loop(1, half, deal, 0)

    def columns_swap():
        drain(rows.at[pl.ds(0, half - 1)], colg_recv)
        push(cols.at[:, core], cols.at[:, core], colx_send, colx_recv, other)

    def inverse_swap():
        drain(inv.at[pl.ds(0, half - 1), 0], ig_recv)
        push(inv.at[:, core], inv.at[:, core], ix_send, ix_recv, other)

    ring_step(0)
    fisher_scatter()
    columns_hop()
    fisher_share()
    ring_step(1)
    columns_along()
    carry = fisher_matrix()
    ring_step(2)
    carry = lax.fori_loop(0, 8, block_step, carry)
    inverse_along(carry[1])
    columns_gather()
    ring_step(3)
    ring_step(4)
    inverse_gather()
    ring_step(5)
    ring_step(6)
    inverse_swap()
    ring_step(7)
    columns_swap()
    drain(inv.at[:, 0], ix_recv)
    drain(cols.at[:, 0], colx_recv)

    wide = lax.broadcasted_iota(jnp.int32, (BW, 256), 1)

    def whiten_plane(k):
        lower = inv[:, :, k].reshape(2, BW, 128)
        zero = jnp.zeros((BW, 128), F32)
        both = [
            jnp.concatenate([lower[0], zero], axis=1),
            jnp.concatenate([zero, lower[1]], axis=1),
        ]
        matrix = jnp.concatenate(
            [jnp.where(wide // BW == i, both[i // 2], 0.0) for i in range(4)], axis=0
        )
        high = matrix.astype(BF16)
        rest = (matrix - high.astype(F32)).astype(BF16)
        offset = pl.ds(pl.multiple_of(k * 256, 256), 256)
        slot = spot_of(lax.rem(z // 2 + 3 * (k // 2), half))

        where = (*slot, lax.rem(k, 2))
        values = jnp.concatenate(
            [rows[k].reshape(256, 256), cols[(0, *where)], cols[(1, *where)]], axis=0
        )
        white = lax.dot_general(
            jnp.concatenate([values, values], axis=1),
            jnp.concatenate([high, rest], axis=1),
            NT,
            preferred_element_type=F32,
        ).astype(BF16)
        wrow[:, offset] = white[:256]
        wcol[0, :, offset] = white[256:384]
        wcol[1, :, offset] = white[384:]

    def plane_step(d, _):
        whiten_plane(lax.rem(z + half + 1 + d, n))
        return 0

    lax.fori_loop(0, n - 1, plane_step, 0, unroll=3)
    far = lax.rem(z + half, n)
    for i in range(CHUNKS):
        arrived(far, i)
    whiten_plane(far)

    def product(i):
        return lax.dot_general(wrow[...], wcol[i], NT, preferred_element_type=F32)

    part[...] = product(1 - x_lo)
    give = push(part, precv, p_send, p_recv, across)
    own = product(x_lo)

    drain(rows.at[pl.ds(0, n - 1)], ring_send)

    @pl.when(hop != r)
    def _():
        drain(pre, pre_send)

    for h in range(2):

        @pl.when(here + h != z)
        def _(h=h):
            drain(cols.at[0, 0, 0, 0], col_send.at[h])

    drain(fsend.at[pl.ds(0, n - 1)], rs_send)
    drain(full.at[pl.ds(0, n - 1)], ag_send)
    drain(linv.at[pl.ds(0, n - 1)], ze_send)
    drain(rows.at[pl.ds(0, half - 1)], colg_send)
    drain(inv.at[pl.ds(0, half - 1), 0], ig_send)
    drain(cols.at[:, 0], colx_send)
    drain(inv.at[:, 0], ix_send)
    give.wait()
    out_ref[...] = (own + precv[...]) * (n * 512) ** (-0.5)


def solution(mesh):
    n = mesh.shape["row"]
    half = n // 2
    depth = 128 // n

    def per_device(grads):
        dma = pltpu.SemaphoreType.DMA
        return pl.pallas_call(
            functools.partial(kernel, n),
            out_shape=jax.ShapeDtypeStruct((256, 128), F32),
            in_specs=[pl.BlockSpec(memory_space=pltpu.VMEM)],
            out_specs=pl.BlockSpec(memory_space=pltpu.VMEM),
            scratch_shapes=[
                pltpu.VMEM((n, CHUNKS, SIZE, 256), BF16),
                pltpu.VMEM((2, 2, half // 2, 2, 128, 256), BF16),
                pltpu.VMEM((n, depth, 128), F32),
                pltpu.VMEM((n, depth, 128), F32),
                pltpu.VMEM((n, depth, 128), F32),
                pltpu.VMEM((n, depth, 128), F32),
                pltpu.VMEM((half, 2, n, depth, 128), F32),
                pltpu.VMEM((256, 128), F32),
                pltpu.VMEM((256, 128), F32),
                pltpu.VMEM((256, 256), BF16),
                pltpu.VMEM((256, n * 256), BF16),
                pltpu.VMEM((2, 128, n * 256), BF16),
                dma((n, CHUNKS)),
                dma((2,)),
            ]
            + [dma] * 20,
            compiler_params=pltpu.CompilerParams(
                collective_id=0, has_side_effects=True, vmem_limit_bytes=40 * 2**20
            ),
        )(grads)

    return jax.shard_map(
        per_device,
        mesh=mesh,
        in_specs=(P("row", "col"),),
        out_specs=P("row", "col"),
        check_vma=False,
    )
```

```python
import functools

import jax
import jax.numpy as jnp
from jax import lax
from jax.experimental import pallas as pl
from jax.experimental.pallas import tpu as pltpu
from jax.sharding import PartitionSpec as P

BW = 64
CHUNKS = 4
SIZE = 256 // CHUNKS
F32 = jnp.float32
BF16 = jnp.bfloat16
MESH = pl.DeviceIdType.MESH
NT = (((1,), (1,)), ((), ()))
TN = (((0,), (0,)), ((), ()))


def eliminate(blocks, inverse):
    lane = lax.broadcasted_iota(jnp.int32, (1, 1, 8, 128), 3)
    sub = lax.broadcasted_iota(jnp.int32, (1, 1, 8, 128), 2)
    low = lane < BW
    for start in (0, 4):
        four = range(start, start + 4)
        columns = [
            jnp.where(low, blocks[:, :, :, j : j + 1], blocks[:, :, :, BW + j : BW + j + 1])
            for j in four
        ]
        factor = [[None] * 4 for _ in range(4)]
        root = [None] * 4
        for v in range(4):
            for u in range(v, 4):
                entry = columns[v][0:1, :, start + u : start + u + 1, :]
                for w in range(v):
                    entry = entry - factor[u][w] * factor[v][w]
                if u == v:
                    root[v] = lax.rsqrt(entry)
                else:
                    factor[u][v] = entry * root[v]

        def solve(array):
            forward = []
            for u in range(4):
                row = array[0:1, :, start + u : start + u + 1, :]
                for w in range(u):
                    row = row - factor[u][w] * forward[w]
                forward.append(row * root[u])
            back = [None] * 4
            for u in reversed(range(4)):
                row = forward[u]
                for w in range(u + 1, 4):
                    row = row - factor[w][u] * back[w]
                back[u] = row * root[u]
            return forward, back

        _, take = solve(blocks)
        done, other = solve(inverse)
        columns = [
            jnp.concatenate([jnp.where(sub > start + 3, column[0:1], 0.0), column[1:]], axis=0)
            for column in columns
        ]
        for v in range(4):
            blocks = blocks - columns[v] * take[v]
            inverse = inverse - columns[v] * other[v]
        top = inverse[0:1]
        for u in range(4):
            top = jnp.where(sub == start + u, done[u], top)
        inverse = jnp.concatenate([top, inverse[1:]], axis=0)
    return blocks, inverse


def kernel(
    n,
    g_ref,
    out_ref,
    rows,
    cols,
    fsend,
    frecv,
    full,
    linv,
    inv,
    part,
    precv,
    pre,
    wrow,
    wcol,
    ring_recv,
    col_send,
    p_send,
    p_recv,
    ring_send,
    pre_send,
    pre_recv,
    col_recv,
    colg_send,
    colg_recv,
    colx_send,
    colx_recv,
    rs_send,
    rs_recv,
    ag_send,
    ag_recv,
    ze_send,
    ze_recv,
    ig_send,
    ig_recv,
    ix_send,
    ix_recv,
):
    r = lax.axis_index("row")
    c = lax.axis_index("col")
    half = n // 2
    quad = half // 2
    x_lo = c // n
    z = lax.rem(c, n)
    x_hi = r // half
    q = lax.rem(r, half)
    y = q // 2
    pair = r // 2
    core = lax.rem(r, 2)
    depth = 128 // n

    def at(row, plane):
        return {"row": row, "col": x_lo * n + plane}

    across = {"row": r, "col": (1 - x_lo) * n + z}

    barrier = pltpu.get_barrier_semaphore()

    def greet(d, _):
        pl.semaphore_signal(barrier, 1, device_id=at(lax.rem(r + d, n), z), device_id_type=MESH)
        pl.semaphore_signal(barrier, 1, device_id=at(r, lax.rem(z + d, n)), device_id_type=MESH)
        return 0

    lax.fori_loop(1, n, greet, 0)
    pl.semaphore_signal(barrier, 1, device_id=across, device_id_type=MESH)
    pl.semaphore_wait(barrier, 2 * (n - 1) + 1)

    def push(source, target, send_sem, recv_sem, device):
        copy = pltpu.make_async_remote_copy(
            src_ref=source,
            dst_ref=target,
            send_sem=send_sem,
            recv_sem=recv_sem,
            device_id=device,
            device_id_type=MESH,
        )
        copy.start()
        return copy

    def drain(ref, sem):
        pltpu.make_async_copy(ref, ref, sem).wait()

    def keep_or_push(local, source, target, send_sem, recv_sem, device):
        @pl.when(local)
        def _():
            pltpu.make_async_copy(source, target, recv_sem).start()

        @pl.when(jnp.logical_not(local))
        def _():
            push(source, target, send_sem, recv_sem, device)

    right = lax.rem(z + 1, n)
    left = lax.rem(z + n - 1, n)

    def arrived(slot, chunk):
        drain(rows.at[slot, chunk], ring_recv.at[slot, chunk])

    def ring_step(t):
        if t >= half:
            return
        back = lax.rem(z - t + n, n)
        ahead = lax.rem(z + t, n)
        for i in range(CHUNKS):
            for slot, chunk, plane in ((back, i, right), (ahead, CHUNKS - 1 - i, left)):
                source = rows.at[slot, chunk]
                if t == 0:
                    source = g_ref.at[pl.ds(chunk * SIZE, SIZE)]
                else:
                    arrived(slot, chunk)
                if t < half - 1 or i < CHUNKS // 2:
                    push(
                        source,
                        rows.at[slot, chunk],
                        ring_send,
                        ring_recv.at[slot, chunk],
                        at(r, plane),
                    )

    lane = lax.broadcasted_iota(jnp.int32, (BW, 128), 1)
    line = lax.broadcasted_iota(jnp.int32, (128, 128), 0)
    place = lax.broadcasted_iota(jnp.int32, (128, 128), 1)
    unit = (lax.rem(line, BW) == lax.rem(place, BW)).astype(F32)
    other = at(r + 1 - 2 * core, z)

    def fisher_scatter():
        gram = lax.dot_general(g_ref[...], g_ref[...], TN, preferred_element_type=F32)
        packed = jnp.concatenate(
            [
                jnp.where(
                    lane < BW,
                    gram[128 * m : 128 * m + BW, 128 * m : 128 * m + 128],
                    gram[128 * m + BW : 128 * m + 128, 128 * m : 128 * m + 128],
                )
                for m in range(2)
            ],
            axis=0,
        )
        fsend[...] = packed.reshape(n, depth, 128)

        def scatter(d, _):
            to = lax.rem(r + d, n)
            push(fsend.at[to], frecv.at[r], rs_send, rs_recv, at(to, z))
            return 0

        lax.fori_loop(1, n, scatter, 0)
        frecv[r] = fsend[r]

    def spot_of(m):
        if quad == 1:
            return m, 0
        return lax.rem(m // 2, 2), m // 4 * 2 + lax.rem(m, 2)

    hop_core, hop_y = spot_of(lax.rem(q + 3 * (z // 2), half))
    hop = x_hi * half + hop_y * 2 + hop_core
    me = core if quad == 1 else y // 2 * 4 + core * 2 + lax.rem(y, 2)

    def columns_hop():
        keep_or_push(hop == r, g_ref, pre, pre_send, pre_recv, at(hop, z))
        rows[z] = g_ref[...].reshape(CHUNKS, SIZE, 256)

    def fisher_share():
        drain(frecv.at[pl.ds(0, n - 1)], rs_recv)
        total = frecv[0]
        for i in range(1, n):
            total = total + frecv[i]
        full[r] = total

        def share(d, _):
            push(full.at[r], full.at[r], ag_send, ag_recv, at(lax.rem(r + d, n), z))
            return 0

        lax.fori_loop(1, n, share, 0)

    here = 2 * lax.rem(me + (4 * half - 3) * (z // 2), half)
    spot = cols.at[x_hi, core, y]

    def columns_along():
        drain(pre, pre_recv)
        for h in range(2):
            keep_or_push(
                here + h == z,
                pre.at[pl.ds(128 * h, 128)],
                spot.at[lax.rem(z, 2)],
                col_send.at[h],
                col_recv,
                at(r, here + h),
            )

    def fisher_matrix():
        drain(full.at[pl.ds(0, n - 1)], ag_recv)
        fisher = full[...].reshape(128, 128) * (1.0 / (n * 256)) + 0.1 * unit
        return split(fisher), split(unit)

    def split(array):
        array = array.reshape(2, 8, 8, 128)
        return jnp.stack([array[:, i] for i in range(8)], axis=0)

    def block_step(b, carry):
        blocks, inverse = eliminate(*carry)
        blocks = pltpu.roll(blocks.reshape(128, 128), 120, 1).reshape(8, 2, 8, 128)
        return (
            jnp.concatenate([blocks[1:], jnp.zeros_like(blocks[:1])], axis=0),
            jnp.concatenate([inverse[1:], inverse[:1]], axis=0),
        )

    def inverse_along(inverse):
        whole = jnp.concatenate([inverse[i, m] for m in range(2) for i in range(8)], axis=0)
        linv[...] = whole.reshape(n, depth, 128)
        inv[pair, core, z] = linv[r]

        def spread(d, _):
            push(linv.at[r], inv.at[pair, core, z], ze_send, ze_recv, at(r, lax.rem(z + d, n)))
            return 0

        lax.fori_loop(1, n, spread, 0)

    def columns_gather():
        drain(spot, col_recv)

        def relay(d, _):
            push(spot, spot, colg_send, colg_recv, at(lax.rem(r + 2 * d, n), z))
            return 0

        lax.fori_loop(1, half, relay, 0)

    def inverse_gather():
        drain(inv.at[0, 0, pl.ds(0, n - 1)], ze_recv)

        def deal(d, _):
            mine = inv.at[pair, core]
            push(mine, mine, ig_send, ig_recv, at(lax.rem(r + 2 * d, n), z))
            return 0

        lax.fori_loop(1, half, deal, 0)

    def columns_swap():
        drain(rows.at[pl.ds(0, half - 1)], colg_recv)
        push(cols.at[:, core], cols.at[:, core], colx_send, colx_recv, other)

    def inverse_swap():
        drain(inv.at[pl.ds(0, half - 1), 0], ig_recv)
        push(inv.at[:, core], inv.at[:, core], ix_send, ix_recv, other)

    ring_step(0)
    fisher_scatter()
    columns_hop()
    fisher_share()
    ring_step(1)
    columns_along()
    carry = fisher_matrix()
    ring_step(2)
    carry = lax.fori_loop(0, 5, block_step, carry)
    ring_step(3)
    carry = lax.fori_loop(5, 8, block_step, carry)
    inverse_along(carry[1])
    columns_gather()
    ring_step(4)
    inverse_gather()
    ring_step(5)
    ring_step(6)
    inverse_swap()
    ring_step(7)
    columns_swap()
    drain(inv.at[:, 0], ix_recv)
    drain(cols.at[:, 0], colx_recv)

    wide = lax.broadcasted_iota(jnp.int32, (BW, 256), 1)

    def whiten_plane(k):
        lower = inv[:, :, k].reshape(2, BW, 128)
        zero = jnp.zeros((BW, 128), F32)
        both = [
            jnp.concatenate([lower[0], zero], axis=1),
            jnp.concatenate([zero, lower[1]], axis=1),
        ]
        matrix = jnp.concatenate(
            [jnp.where(wide // BW == i, both[i // 2], 0.0) for i in range(4)], axis=0
        )
        high = matrix.astype(BF16)
        rest = (matrix - high.astype(F32)).astype(BF16)
        offset = pl.ds(pl.multiple_of(k * 256, 256), 256)
        slot = spot_of(lax.rem(z // 2 + 3 * (k // 2), half))

        where = (*slot, lax.rem(k, 2))
        values = jnp.concatenate(
            [rows[k].reshape(256, 256), cols[(0, *where)], cols[(1, *where)]], axis=0
        )
        white = lax.dot_general(
            jnp.concatenate([values, values], axis=1),
            jnp.concatenate([high, rest], axis=1),
            NT,
            preferred_element_type=F32,
        ).astype(BF16)
        wrow[:, offset] = white[:256]
        wcol[0, :, offset] = white[256:384]
        wcol[1, :, offset] = white[384:]

    def plane_step(d, _):
        whiten_plane(lax.rem(z + half + 1 + d, n))
        return 0

    lax.fori_loop(0, n - 1, plane_step, 0, unroll=3)
    far = lax.rem(z + half, n)
    for i in range(CHUNKS):
        arrived(far, i)
    whiten_plane(far)

    def product(i):
        return lax.dot_general(wrow[...], wcol[i], NT, preferred_element_type=F32)

    part[...] = product(1 - x_lo)
    give = push(part, precv, p_send, p_recv, across)
    own = product(x_lo)

    drain(rows.at[pl.ds(0, n - 1)], ring_send)

    @pl.when(hop != r)
    def _():
        drain(pre, pre_send)

    for h in range(2):

        @pl.when(here + h != z)
        def _(h=h):
            drain(cols.at[0, 0, 0, 0], col_send.at[h])

    drain(fsend.at[pl.ds(0, n - 1)], rs_send)
    drain(full.at[pl.ds(0, n - 1)], ag_send)
    drain(linv.at[pl.ds(0, n - 1)], ze_send)
    drain(rows.at[pl.ds(0, half - 1)], colg_send)
    drain(inv.at[pl.ds(0, half - 1), 0], ig_send)
    drain(cols.at[:, 0], colx_send)
    drain(inv.at[:, 0], ix_send)
    give.wait()
    out_ref[...] = (own + precv[...]) * (n * 512) ** (-0.5)


def solution(mesh):
    n = mesh.shape["row"]
    half = n // 2
    depth = 128 // n

    def per_device(grads):
        dma = pltpu.SemaphoreType.DMA
        return pl.pallas_call(
            functools.partial(kernel, n),
            out_shape=jax.ShapeDtypeStruct((256, 128), F32),
            in_specs=[pl.BlockSpec(memory_space=pltpu.VMEM)],
            out_specs=pl.BlockSpec(memory_space=pltpu.VMEM),
            scratch_shapes=[
                pltpu.VMEM((n, CHUNKS, SIZE, 256), BF16),
                pltpu.VMEM((2, 2, half // 2, 2, 128, 256), BF16),
                pltpu.VMEM((n, depth, 128), F32),
                pltpu.VMEM((n, depth, 128), F32),
                pltpu.VMEM((n, depth, 128), F32),
                pltpu.VMEM((n, depth, 128), F32),
                pltpu.VMEM((half, 2, n, depth, 128), F32),
                pltpu.VMEM((256, 128), F32),
                pltpu.VMEM((256, 128), F32),
                pltpu.VMEM((256, 256), BF16),
                pltpu.VMEM((256, n * 256), BF16),
                pltpu.VMEM((2, 128, n * 256), BF16),
                dma((n, CHUNKS)),
                dma((2,)),
            ]
            + [dma] * 20,
            compiler_params=pltpu.CompilerParams(
                collective_id=0, has_side_effects=True, vmem_limit_bytes=40 * 2**20
            ),
        )(grads)

    return jax.shard_map(
        per_device,
        mesh=mesh,
        in_specs=(P("row", "col"),),
        out_specs=P("row", "col"),
        check_vma=False,
    )
```
